32 devices in a mesh: ctx: 8 (over z, y), dp: 4 (over x, core).
Axes of the slice: x: 2, y: 2, z: 4, core: 2. Of those that a mesh axis runs over, the one named last changes fastest.
Arguments:
- queries: bfloat16 [4, 2048, 2048], P('dp', 'ctx'), may hold values from -9 to 9, as said below
- keys: bfloat16 [4, 2048, 512], P('dp', 'ctx'), may hold values from -9 to 9
- values: bfloat16 [4, 2048, 512], P('dp', 'ctx'), may hold values from -20 to 20
- hyena_x1: bfloat16 [4, 2048, 2048], P('dp', 'ctx'), may hold values from -6 to 6
- hyena_x2: bfloat16 [4, 2048, 2048], P('dp', 'ctx'), may hold values from -6 to 6
- hyena_v: bfloat16 [4, 2048, 2048], P('dp', 'ctx'), may hold values from -6 to 6
- filters: bfloat16 [128, 128], replicated, may hold values from -6 to 6
- panels: bfloat16 [4, 256, 4096], P('dp', 'ctx'), may hold values from -6 to 6
- owner: int32 [4, 256, 1], P('dp', 'ctx'), may hold values from 0 to 3; in each aligned block of 32 rows (0 to 31, 32 to 63, ..., all dimensions but the last counted through in order) at most 32 rows name the same one
- step_rows: int32 [4, 256], P('dp', 'ctx'), may hold values from 0 to 2047, as said below
Outputs:
- mixed: bfloat16 [4, 2048, 2048], P('dp', 'ctx')
The draws below stay inside these ranges and needn't reach their ends.
Inputs may be any that keep to these rules, and one draw needn't show every extreme that they name: In the hidden draw a few queries are aligned with two earlier keys; the normal draw stays within 6. `step_rows`: the panels held by the device at index c of ctx belong to positions c * 256 to (c + 1) * 256 - 1 of their traces. Of the panels on one device, at most 32 have the same owner, and that bound is reached.
All inputs are finite; a program needn't handle non-finite values.
Results may differ from the reference program's by a relative error of at most 0.0055.
Values may be sent and summed in bfloat16 or wider, within the bound.
A program may use at most 128 MiB of HBM per device.

```python
import math
import jax
import jax.numpy as jnp
import numpy as np
from jax import lax

HEADS = 16
KV_HEADS = 4
HEAD_DIM = 128
TAPS = 128
GROUP = 16
TOK_DEV = 256
PAN_DEV = 32
CHANNELS = 2048
FGROUPS = 128
HINT = 4096
SEQ = 2048
TRACES = 4
PANELS = 256
CAP = 32
N_DP = 4


def base_values(key, shape):
    return jnp.clip(jax.random.normal(key, shape, jnp.float32), -6.0, 6.0)


def draw_queries(key, part):
    base = base_values(jax.random.fold_in(key, 1), (TRACES, SEQ, HEADS * HEAD_DIM))
    return base.astype(jnp.bfloat16)


def draw_keys(key, part):
    base = base_values(jax.random.fold_in(key, 2), (TRACES, SEQ, KV_HEADS * HEAD_DIM))
    return base.astype(jnp.bfloat16)


def draw_filters(key, part):
    span = jnp.exp(jax.random.uniform(jax.random.fold_in(key, 3), (FGROUPS, 1), jnp.float32, math.log(8.0), math.log(1000.0)))
    rate = jnp.exp(-1.0 / span)
    norm = jnp.sqrt((1.0 - rate ** (2 * TAPS)) / (1.0 - rate * rate))
    lags = jnp.arange(TAPS, dtype=jnp.float32)[None, :]
    noise = base_values(jax.random.fold_in(key, 4), (FGROUPS, TAPS))
    return (noise * rate ** lags / norm).astype(jnp.bfloat16)


def draw_step_rows(key, part):
    offset = jax.random.randint(jax.random.fold_in(key, 5), (TRACES, PANELS), 0, TOK_DEV)
    within = jnp.arange(PANELS, dtype=jnp.int32) % PAN_DEV
    offset = jnp.where(within[None, :] == 0, TOK_DEV - 1, jnp.where(within[None, :] == 1, 0, offset))
    shard = jnp.arange(PANELS, dtype=jnp.int32) // PAN_DEV
    return (shard * TOK_DEV)[None, :] + offset


def levels(own_key, extent, split, low, high):
    def one(axis_at, blocks):
        draws = jax.random.uniform(jax.random.fold_in(jax.random.fold_in(own_key, 6), axis_at), (blocks,), jnp.float32, low / len(split), high / len(split))
        return jnp.repeat(jnp.exp(draws), extent[axis_at] // blocks).reshape((-1,) + (1,) * (len(extent) - axis_at - 1))

    gain = one(*split[0])
    for cut in split[1:]:
        gain = gain * one(*cut)
    return gain


def routed_block(rng, own, number, rows, amount, top, reach, skew):
    order = jax.random.permutation(rng, amount)
    packed, common = load_shares(amount, rows * top, reach, skew, True), load_shares(amount, rows * top, reach, skew, False)
    places = jnp.arange(amount)

    def named(sizes, turn):
        used = int((sizes > 0).sum())
        fixed = max(1, used // 4)
        moved = fixed + (places - fixed + turn * (used - fixed)) % max(1, amount - fixed)
        return jnp.zeros((amount,), jnp.int32).at[order[jnp.where(places < fixed, places, moved)]].set(jnp.asarray(sizes, jnp.int32))

    sizes = jnp.where(number % 4 == 0, named(packed, number // 4), named(common, number - number // 4 - 1))
    mixed = jax.random.permutation(jax.random.fold_in(own, 3), amount)
    donor, sink = mixed[0:amount // 2 * 2:2], mixed[1:amount // 2 * 2:2]
    margin = jnp.minimum(sizes[donor] - 1, reach - sizes[sink]) // 2
    margin = jnp.where((donor == order[0]) | (sink == order[0]) | (sizes[sink] == 0), 0, jnp.maximum(margin, 0))
    moved = jax.random.randint(jax.random.fold_in(own, 4), (amount // 2,), 0, 1 << 20) % (margin + 1)
    sizes = sizes.at[donor].add(-moved).at[sink].add(moved)
    labels = jnp.searchsorted(jnp.cumsum(sizes), jnp.arange(rows * top), side="right").astype(jnp.int32)
    table = labels.reshape(top, rows).T
    table = table[jax.random.permutation(jax.random.fold_in(own, 1), rows)]
    turn = jax.random.randint(jax.random.fold_in(own, 2), (rows, 1), 0, top)
    return jnp.take_along_axis(table, (jnp.arange(top)[None, :] + turn) % top, axis=1)


def load_shares(count, total, most, lean, full):
    weights = [(1 << 20) // math.isqrt(grade ** lean) + 1 for grade in range(1, count + 1)]
    largest = most if full else min(most, max(-(-total // count), total * weights[0] // sum(weights)))
    least = 1 if total - largest >= count - 1 else 0
    given, spare = [largest] + [least] * (count - 1), total - largest - least * (count - 1)
    while spare > 0:
        movable = [i for i in range(1, count) if given[i] < largest] or [i for i in range(1, count) if given[i] < most]
        whole, budget = sum([weights[i] for i in movable]), spare
        for i in movable:
            more = min(most - given[i], max(1, budget * weights[i] // whole), spare)
            given[i] = given[i] + more
            spare = spare - more
    return np.array(given)


def gaussian(own_key, shape, spread, most, cuts=(), kind=jnp.bfloat16):
    entries = spread * jax.random.normal(own_key, shape, jnp.float32)
    if cuts:
        entries = entries * levels(own_key, shape, cuts, -0.22, 0.18)
    return jnp.clip(entries, -most, most).astype(kind)


def setup_inputs(seed: int = 0) -> dict:
    key_of = jax.random.split(jax.random.key(seed), 11)
    queries = draw_queries(jax.random.fold_in(key_of[10], 71), 0)
    keys = draw_keys(jax.random.fold_in(key_of[10], 71), 0)
    values = gaussian(key_of[2], (TRACES, SEQ, KV_HEADS * HEAD_DIM), 4.0, 20.0, ((0, 4), (1, 8)))
    hyena_x1 = gaussian(key_of[3], (TRACES, SEQ, CHANNELS), 1.0, 6.0, ((0, 4), (1, 8)))
    hyena_x2 = gaussian(key_of[4], (TRACES, SEQ, CHANNELS), 1.0, 6.0, ((0, 4), (1, 8)))
    hyena_v = gaussian(key_of[5], (TRACES, SEQ, CHANNELS), 1.0, 6.0, ((0, 4), (1, 8)))
    filters = draw_filters(jax.random.fold_in(key_of[10], 71), 0)
    panels = gaussian(key_of[7], (TRACES, PANELS, HINT), 1.0, 6.0, ((0, 4), (1, 8)))
    owner_keys = jax.random.split(jax.random.fold_in(key_of[8], 1), TRACES * PANELS // PAN_DEV)
    owner_turns = jax.random.permutation(jax.random.fold_in(key_of[8], 3), TRACES * PANELS // PAN_DEV)
    owner = jax.vmap(lambda own, number: routed_block(jax.random.fold_in(key_of[8], 2), own, number, PAN_DEV, N_DP, 1, CAP, 2))(owner_keys, owner_turns).reshape((TRACES, PANELS, 1))
    step_rows = draw_step_rows(jax.random.fold_in(key_of[10], 71), 0)
    return dict(queries=queries, keys=keys, values=values, hyena_x1=hyena_x1, hyena_x2=hyena_x2, hyena_v=hyena_v, filters=filters, panels=panels, owner=owner, step_rows=step_rows)


NEG = -1e30


def conv_trace(u_rows, filters):
    width = u_rows.shape[1]
    nblk = SEQ // TAPS
    ext = jnp.concatenate([jnp.zeros((TAPS, width), jnp.float32), u_rows.astype(jnp.float32)], 0)
    blocks = ext.reshape(nblk + 1, TAPS, FGROUPS, GROUP)
    lag = jnp.arange(TAPS, dtype=jnp.int32)[:, None] - jnp.arange(TAPS, dtype=jnp.int32)[None, :]
    taps_f = filters.astype(jnp.float32)
    lower = jnp.where(lag >= 0, taps_f[:, jnp.clip(lag, 0, TAPS - 1)], jnp.float32(0.0))
    upper = jnp.where(lag < 0, taps_f[:, jnp.clip(lag + TAPS, 0, TAPS - 1)], jnp.float32(0.0))
    hi = lax.Precision.HIGHEST
    conv = jnp.einsum("gij,bjgc->bigc", lower, blocks[1:], precision=hi)
    conv = conv + jnp.einsum("gij,bjgc->bigc", upper, blocks[:-1], precision=hi)
    return conv.reshape(SEQ, width)


def attend_trace(q_rows, k_rows, v_rows):
    grp = HEADS // KV_HEADS
    qblk = math.gcd(SEQ, 512)
    scale = HEAD_DIM ** -0.5
    k_f = k_rows.astype(jnp.float32).reshape(SEQ, KV_HEADS, HEAD_DIM)
    v_f = v_rows.astype(jnp.float32).reshape(SEQ, KV_HEADS, HEAD_DIM)
    q_blocks = q_rows.reshape(SEQ // qblk, qblk, KV_HEADS, grp, HEAD_DIM)
    key_pos = jnp.arange(SEQ, dtype=jnp.int32)
    hi = lax.Precision.HIGHEST

    def one_block(item):
        index, q_blk = item
        scores = jnp.einsum("rhgd,khd->hgrk", q_blk.astype(jnp.float32), k_f, precision=hi) * scale
        q_pos = index * qblk + jnp.arange(qblk, dtype=jnp.int32)
        allowed = key_pos[None, :] <= q_pos[:, None]
        scores = jnp.where(allowed, scores, NEG)
        top = jnp.max(scores, axis=-1)
        expo = jnp.where(allowed, jnp.exp(scores - top[..., None]), jnp.float32(0.0))
        total = jnp.sum(expo, axis=-1)
        weight = expo.astype(jnp.bfloat16).astype(jnp.float32)
        numer = jnp.einsum("hgrk,khd->hgrd", weight, v_f, precision=hi)
        out = numer / total[..., None]
        return out.transpose(2, 0, 1, 3).reshape(qblk, HEADS * HEAD_DIM)

    outs = lax.map(one_block, (jnp.arange(SEQ // qblk, dtype=jnp.int32), q_blocks))
    return outs.reshape(SEQ, HEADS * HEAD_DIM)


def reference(queries, keys, values, hyena_x1, hyena_x2, hyena_v, filters, panels, owner, step_rows):
    def one_trace(item):
        q_rows, k_rows, v_rows, first, second, third = item
        u_rows = (first.astype(jnp.float32) * third.astype(jnp.float32)).astype(jnp.bfloat16)
        hyena = second.astype(jnp.float32) * conv_trace(u_rows, filters)
        return hyena + attend_trace(q_rows, k_rows, v_rows)

    mixed = lax.map(one_trace, (queries, keys, values, hyena_x1, hyena_x2, hyena_v))
    gates = panels[:, :, :CHANNELS].astype(jnp.float32)
    vals = panels[:, :, CHANNELS:].astype(jnp.float32)
    hint = (jax.nn.sigmoid(gates) * vals).astype(jnp.bfloat16).astype(jnp.float32)
    mixed = mixed.at[owner[:, :, 0], step_rows].add(hint)
    return mixed.astype(jnp.bfloat16)
```

```python
import functools
import math

import jax
import jax.numpy as jnp
from jax import lax
from jax.experimental import pallas as pl
from jax.experimental.pallas import tpu as pltpu
from jax.sharding import PartitionSpec as P

HEAD_DIM = 128
LANES = 128
NEG = -1e30
MESH = pl.DeviceIdType.MESH
F32 = jnp.float32
BF16 = jnp.bfloat16


def kernel(
    n_ctx, n_dp,
    q_ref, k_ref, v_ref, x1_ref, x2_ref, hv_ref, filt_ref, pan_ref, own_ref, step_ref,
    out_ref,
    kv, uext, hfwd, hint, code, toep, conv, m_ref, l_ref, o_ref,
    zsend, zrecv, ysend, yrecv, hsend, hrecv, csend, crecv,
):
    tok, width = q_ref.shape
    kv_width = k_ref.shape[1]
    heads = width // HEAD_DIM
    kv_heads = kv_width // HEAD_DIM
    grp = heads // kv_heads
    fgroups, taps = filt_ref.shape
    chan = width // fgroups
    count = pan_ref.shape[0]
    seq = tok * n_ctx
    n_z = n_ctx // 2
    c = lax.axis_index("ctx")
    d = lax.axis_index("dp")
    z = c // 2
    y = c % 2
    low = y == 0
    high = y == 1
    has_up = z < n_z - 1
    has_down = z > 0
    partner = (2 * z + 1 - y, d)
    up = (jnp.minimum(c + 2, n_ctx - 1), d)
    down = (jnp.maximum(c - 2, 0), d)

    barrier = pltpu.get_barrier_semaphore()
    pl.semaphore_signal(barrier, 1, device_id=partner, device_id_type=MESH)
    for s in range(1, n_dp):
        pl.semaphore_signal(barrier, 1, device_id=(c, (d + s) % n_dp), device_id_type=MESH)

    @pl.when(has_up)
    def _():
        pl.semaphore_signal(barrier, 1, device_id=up, device_id_type=MESH)

    @pl.when(has_down)
    def _():
        pl.semaphore_signal(barrier, 1, device_id=down, device_id_type=MESH)

    kv[c, :, :kv_width] = k_ref[...]
    kv[c, :, kv_width:] = v_ref[...]
    uext[taps:, :] = x1_ref[...] * hv_ref[...]

    @pl.when(c == 0)
    def _():
        uext[:taps, :] = jnp.zeros((taps, width), BF16)

    pl.semaphore_wait(
        barrier, n_dp + has_up.astype(jnp.int32) + has_down.astype(jnp.int32)
    )

    def remote(src, dst, s_sem, r_sem, who):
        return pltpu.make_async_remote_copy(
            src_ref=src, dst_ref=dst, send_sem=s_sem, recv_sem=r_sem,
            device_id=who, device_id_type=MESH,
        )

    def z_copy(hi):
        slot = kv.at[2 * hi + y]
        return remote(slot, slot, zsend.at[hi], zrecv.at[hi], up)

    def z_extra_block(hi):
        slot = kv.at[2 * hi]
        return remote(slot, slot, zsend.at[n_z], zrecv.at[n_z], up)

    halo_out = uext.at[pl.ds(tok, taps)]
    halo_in = uext.at[pl.ds(0, taps)]

    def z_extra_halo():
        return remote(hfwd, halo_in, zsend.at[n_z], zrecv.at[n_z], up)

    def y_copy(hi):
        slot = kv.at[2 * hi + y]
        return remote(slot, slot, ysend.at[hi], yrecv.at[hi], partner)

    def y_arrival(hi):
        slot = kv.at[2 * hi + 1 - y]
        return remote(slot, slot, ysend.at[hi], yrecv.at[hi], partner)

    def y_halo_low():
        return remote(halo_out, halo_in, ysend.at[n_z], yrecv.at[n_z], partner)

    def y_halo_high():
        return remote(halo_out, hfwd, ysend.at[n_z], yrecv.at[n_z], partner)

    @pl.when(has_up)
    def _():
        z_copy(z).start()

    @pl.when(low)
    def _():
        y_copy(z).start()

    @pl.when(high & has_up)
    def _():
        y_halo_high().start()

    half = pan_ref.shape[1] // 2
    gates = pan_ref[:, :half].astype(F32)
    hint[d] = (jax.nn.sigmoid(gates) * pan_ref[:, half:].astype(F32)).astype(BF16)
    eye = lax.broadcasted_iota(jnp.int32, (count, count), 0) == lax.broadcasted_iota(
        jnp.int32, (count, count), 1
    )
    steps = jnp.sum(
        jnp.where(eye, jnp.broadcast_to(step_ref[...], (count, count)), 0), axis=1, keepdims=True
    )
    code[d] = jnp.broadcast_to(own_ref[...] * seq + steps, (count, LANES))

    def hint_copy(s, me):
        return remote(
            hint.at[me], hint.at[me], hsend.at[s], hrecv.at[s], (c, (d + s) % n_dp)
        )

    def code_copy(s, me):
        return remote(
            code.at[me], code.at[me], csend.at[s], crecv.at[s], (c, (d + s) % n_dp)
        )

    for s in range(1, n_dp):
        hint_copy(s, d).start()
        code_copy(s, d).start()

    factor = HEAD_DIM ** -0.5 * math.log2(math.e)

    def attend(slot, diagonal=False):
        def one(kh, carry):
            k_at = pl.ds(pl.multiple_of(kh * HEAD_DIM, HEAD_DIM), HEAD_DIM)
            v_at = pl.ds(pl.multiple_of(kv_width + kh * HEAD_DIM, HEAD_DIM), HEAD_DIM)
            key = kv[slot, :, k_at]
            val = kv[slot, :, v_at]
            for g in range(grp):
                h = kh * grp + g
                query = q_ref[:, pl.ds(pl.multiple_of(h * HEAD_DIM, HEAD_DIM), HEAD_DIM)]
                score = lax.dot_general(
                    key, query, (((1,), (1,)), ((), ())), preferred_element_type=F32
                ) * factor
                if diagonal:
                    keep = lax.broadcasted_iota(jnp.int32, (tok, tok), 0) <= (
                        lax.broadcasted_iota(jnp.int32, (tok, tok), 1)
                    )
                    score = jnp.where(keep, score, NEG)
                    top = jnp.max(score, axis=0, keepdims=True)
                else:
                    before = m_ref[h]
                    top = jnp.maximum(before, jnp.max(score, axis=0, keepdims=True))
                expo = jnp.exp2(score - top)
                total = jnp.sum(expo, axis=0, keepdims=True)
                part = lax.dot_general(
                    val, expo.astype(BF16), (((0,), (0,)), ((), ())), preferred_element_type=F32
                )
                if diagonal:
                    l_ref[h] = total
                    o_ref[h] = part
                else:
                    shrink = jnp.exp2(before - top)
                    l_ref[h] = l_ref[h] * shrink + total
                    o_ref[h] = o_ref[h] * shrink + part
                m_ref[h] = top
            return carry

        lax.fori_loop(0, kv_heads, one, 0)

    attend(c, diagonal=True)

    lag_at = lax.broadcasted_iota(jnp.int32, (taps, 2 * taps), 0)
    col_at = lax.broadcasted_iota(jnp.int32, (taps, 2 * taps), 1)
    flip = jnp.where(lag_at == taps - col_at, 1.0, 0.0).astype(BF16)
    per_tile = LANES // chan
    n_tiles = width // LANES
    lane_group = lax.broadcasted_iota(jnp.int32, (taps, LANES), 1) // chan
    n_blk = tok // taps

    def pick(prod, col):
        res = prod[:taps, col]
        for g in range(1, per_tile):
            res = jnp.where(lane_group == g, prod[g * taps:(g + 1) * taps, col], res)
        return res

    def conv_tile(tile, carry):
        at = pl.ds(pl.multiple_of(tile * LANES, LANES), LANES)
        rows = filt_ref[pl.ds(pl.multiple_of(tile * per_tile, per_tile), per_tile), :]
        first = jnp.dot(rows, flip, preferred_element_type=F32)
        for g in range(per_tile):
            row = jnp.broadcast_to(first[g:g + 1, :], (taps, 2 * taps))
            toep[tile, g * taps:(g + 1) * taps, :] = pltpu.roll(
                row, 0, 1, stride=1, stride_axis=0
            ).astype(BF16)
        lower = toep[tile, :, taps:]
        prod = jnp.dot(lower, uext[taps:2 * taps, at], preferred_element_type=F32)
        conv[:taps, at] = pick(prod, slice(None))
        for b in range(1, n_blk):
            prod = jnp.dot(
                toep[tile], uext[b * taps:(b + 2) * taps, at], preferred_element_type=F32
            )
            conv[b * taps:(b + 1) * taps, at] = pick(prod, slice(None))
        return carry

    lax.fori_loop(0, n_tiles, conv_tile, 0)

    @pl.when(low)
    def _():
        y_halo_low().start()

    @pl.when(high)
    def _():
        y_arrival(z).wait_recv()
        attend(2 * z)

    def step(k, carry):
        hi = z - k
        z_copy(hi).wait_recv()

        @pl.when(has_up)
        def _():
            z_copy(hi).start()

        @pl.when(high | (k >= 2))
        def _():
            y_copy(hi).start()

        attend(2 * hi + y)

        @pl.when((k >= 2) & (low | (k >= 3)))
        def _():
            y_arrival(hi + 1).wait_recv()
            attend(2 * (hi + 1) + 1 - y)

        return carry

    lax.fori_loop(1, z + 1, step, 0)

    @pl.when(low & has_up)
    def _():
        y_halo_high().wait_recv()
        z_extra_halo().start()

    @pl.when(high & has_up)
    def _():
        z_extra_block(z).start()

    def conv_halo():
        def tile_step(tile, carry):
            at = pl.ds(pl.multiple_of(tile * LANES, LANES), LANES)
            prod = jnp.dot(
                toep[tile, :, :taps], uext[:taps, at], preferred_element_type=F32
            )
            conv[:taps, at] += pick(prod, slice(None))
            return carry

        lax.fori_loop(0, n_tiles, tile_step, 0)

    @pl.when(high)
    def _():
        y_halo_low().wait_recv()
        conv_halo()

    @pl.when((low & (z >= 1)) | (z >= 2))
    def _():
        y_arrival(0).wait_recv()
        attend(1 - y)

    @pl.when(low & has_down)
    def _():
        z_extra_halo().wait_recv()
        conv_halo()

    @pl.when(high & has_down)
    def _():
        z_extra_block(z - 1).wait_recv()
        attend(2 * (z - 1))

    for s in range(1, n_dp):
        hint_copy(s, (d + n_dp - s) % n_dp).wait_recv()
        code_copy(s, (d + n_dp - s) % n_dp).wait_recv()

    spot = lax.broadcasted_iota(jnp.int32, (n_dp * count, tok), 1) + (d * seq + c * tok)
    codes = code[...].reshape(n_dp * count, LANES)[:, :1]
    landing = jnp.where(codes == spot, 1.0, 0.0).astype(BF16)
    for h in range(heads):
        at = pl.ds(h * HEAD_DIM, HEAD_DIM)
        placed = lax.dot_general(
            landing, hint[:, :, at].reshape(n_dp * count, HEAD_DIM),
            (((0,), (0,)), ((), ())), preferred_element_type=F32,
        )
        normed = (o_ref[h] / l_ref[h]).T
        out_ref[:, at] = (x2_ref[:, at].astype(F32) * conv[:, at] + normed + placed).astype(BF16)

    for s in range(1, n_dp):
        hint_copy(s, d).wait_send()
        code_copy(s, d).wait_send()

    @pl.when(low)
    def _():
        y_copy(z).wait_send()
        y_halo_low().wait_send()

    @pl.when(high & has_up)
    def _():
        y_halo_high().wait_send()
        z_extra_block(z).wait_send()

    @pl.when(low & has_up)
    def _():
        z_extra_halo().wait_send()

    @pl.when(has_up)
    def _():
        z_copy(z).wait_send()

    def drain(k, carry):
        @pl.when(has_up)
        def _():
            z_copy(z - k).wait_send()

        @pl.when(high | (k >= 2))
        def _():
            y_copy(z - k).wait_send()

        return carry

    lax.fori_loop(1, z + 1, drain, 0)


def solution(mesh):
    n_ctx, n_dp = mesh.shape["ctx"], mesh.shape["dp"]

    def per_device(q, k, v, x1, x2, hv, filters, panels, owner, step_rows):
        tok, width = q.shape[1:]
        kv_width = k.shape[2]
        heads = width // HEAD_DIM
        fgroups, taps = filters.shape
        count = panels.shape[1]
        n_z = n_ctx // 2
        dma = pltpu.SemaphoreType.DMA
        vmem = pl.BlockSpec(memory_space=pltpu.VMEM)
        out = pl.pallas_call(
            functools.partial(kernel, n_ctx, n_dp),
            out_shape=jax.ShapeDtypeStruct((tok, width), BF16),
            in_specs=[vmem] * 10,
            out_specs=vmem,
            scratch_shapes=[
                pltpu.VMEM((n_ctx, tok, 2 * kv_width), BF16),
                pltpu.VMEM((taps + tok, width), BF16),
                pltpu.VMEM((taps, width), BF16),
                pltpu.VMEM((n_dp, count, width), BF16),
                pltpu.VMEM((n_dp, count, LANES), jnp.int32),
                pltpu.VMEM((width // LANES, taps * fgroups * LANES // width, 2 * taps), BF16),
                pltpu.VMEM((tok, width), F32),
                pltpu.VMEM((heads, 1, tok), F32),
                pltpu.VMEM((heads, 1, tok), F32),
                pltpu.VMEM((heads, HEAD_DIM, tok), F32),
                dma((n_z + 1,)), dma((n_z + 1,)), dma((n_z + 1,)), dma((n_z + 1,)),
                dma((n_dp,)), dma((n_dp,)), dma((n_dp,)), dma((n_dp,)),
            ],
            compiler_params=pltpu.CompilerParams(
                collective_id=0, has_side_effects=True, vmem_limit_bytes=56 * 2**20
            ),
        )(q[0], k[0], v[0], x1[0], x2[0], hv[0], filters, panels[0], owner[0], step_rows)
        return out[None]

    rows = P("dp", "ctx", None)
    return jax.shard_map(
        per_device,
        mesh=mesh,
        in_specs=(rows,) * 6 + (P(), rows, rows, P("dp", "ctx")),
        out_specs=rows,
        check_vma=False,
    )
```

```python
import functools
import math

import jax
import jax.numpy as jnp
from jax import lax
from jax.experimental import pallas as pl
from jax.experimental.pallas import tpu as pltpu
from jax.sharding import PartitionSpec as P

HEAD_DIM = 128
LANES = 128
NEG = -1e30
CHUNKS = 2
MESH = pl.DeviceIdType.MESH
F32 = jnp.float32
BF16 = jnp.bfloat16


def kernel(
    n_ctx, n_dp,
    q_hbm, k_hbm, v_hbm, x1_hbm, x2_hbm, hv_hbm, filt_ref, pan_hbm, own_ref, step_ref,
    out_ref,
    q_ref, x1_ref, x2_ref, hv_ref, pan_ref,
    kv, uext, hfwd, hint, code, toep, conv, m_ref, l_ref, o_ref,
    zsend, zrecv, ysend, yrecv, hsend, hrecv, csend, crecv, load_sem,
):
    tok, width = q_ref.shape
    kv_width = k_hbm.shape[1]
    part_width = kv_width // CHUNKS
    heads = width // HEAD_DIM
    kv_heads = kv_width // HEAD_DIM
    grp = heads // kv_heads
    fgroups, taps = filt_ref.shape
    chan = width // fgroups
    count = pan_ref.shape[0]
    seq = tok * n_ctx
    n_z = n_ctx // 2
    c = lax.axis_index("ctx")
    d = lax.axis_index("dp")
    z = c // 2
    y = c % 2
    low = y == 0
    high = y == 1
    has_up = z < n_z - 1
    has_down = z > 0
    partner = (2 * z + 1 - y, d)
    up = (jnp.minimum(c + 2, n_ctx - 1), d)
    down = (jnp.maximum(c - 2, 0), d)

    barrier = pltpu.get_barrier_semaphore()
    pl.semaphore_signal(barrier, 1, device_id=partner, device_id_type=MESH)
    for s in range(1, n_dp):
        pl.semaphore_signal(barrier, 1, device_id=(c, (d + s) % n_dp), device_id_type=MESH)

    @pl.when(has_up)
    def _():
        pl.semaphore_signal(barrier, 1, device_id=up, device_id_type=MESH)

    @pl.when(has_down)
    def _():
        pl.semaphore_signal(barrier, 1, device_id=down, device_id_type=MESH)

    def load(src, dst, index):
        return pltpu.make_async_copy(src, dst, load_sem.at[index])

    own_loads = []
    for ch in range(CHUNKS):
        cols = pl.ds(ch * part_width, part_width)
        own_loads.append((
            load(k_hbm.at[:, cols], kv.at[c * CHUNKS + ch, :, pl.ds(0, part_width)], 2 * ch),
            load(
                v_hbm.at[:, cols], kv.at[c * CHUNKS + ch, :, pl.ds(part_width, part_width)],
                2 * ch + 1,
            ),
        ))
    at_sem = 2 * CHUNKS
    load_x1 = load(x1_hbm, x1_ref, at_sem)
    load_hv = load(hv_hbm, hv_ref, at_sem + 1)
    load_pan = load(pan_hbm, pan_ref, at_sem + 2)
    load_q = load(q_hbm, q_ref, at_sem + 3)
    load_x2 = load(x2_hbm, x2_ref, at_sem + 4)
    for pair in own_loads:
        for one_load in pair:
            one_load.start()
    for one_load in (load_x1, load_hv, load_pan, load_q, load_x2):
        one_load.start()

    @pl.when(c == 0)
    def _():
        uext[:taps, :] = jnp.zeros((taps, width), BF16)

    pl.semaphore_wait(
        barrier, n_dp + has_up.astype(jnp.int32) + has_down.astype(jnp.int32)
    )

    def remote(src, dst, s_sem, r_sem, who):
        return pltpu.make_async_remote_copy(
            src_ref=src, dst_ref=dst, send_sem=s_sem, recv_sem=r_sem,
            device_id=who, device_id_type=MESH,
        )

    def z_copy(hi, ch):
        slot = kv.at[(2 * hi + y) * CHUNKS + ch]
        at = hi * CHUNKS + ch
        return remote(slot, slot, zsend.at[at], zrecv.at[at], up)

    last = n_z * CHUNKS

    def z_extra_block(hi, ch):
        slot = kv.at[2 * hi * CHUNKS + ch]
        return remote(slot, slot, zsend.at[last + ch], zrecv.at[last + ch], up)

    halo_out = uext.at[pl.ds(tok, taps)]
    halo_in = uext.at[pl.ds(0, taps)]

    def z_extra_halo():
        return remote(hfwd, halo_in, zsend.at[last], zrecv.at[last], up)

    def y_copy(hi, ch):
        slot = kv.at[(2 * hi + y) * CHUNKS + ch]
        at = hi * CHUNKS + ch
        return remote(slot, slot, ysend.at[at], yrecv.at[at], partner)

    def y_arrival(hi, ch):
        slot = kv.at[(2 * hi + 1 - y) * CHUNKS + ch]
        at = hi * CHUNKS + ch
        return remote(slot, slot, ysend.at[at], yrecv.at[at], partner)

    def y_halo_low():
        return remote(halo_out, halo_in, ysend.at[last], yrecv.at[last], partner)

    def y_halo_high():
        return remote(halo_out, hfwd, ysend.at[last], yrecv.at[last], partner)

    for ch in range(CHUNKS):
        for one_load in own_loads[ch]:
            one_load.wait()

        @pl.when(has_up)
        def _():
            z_copy(z, ch).start()

        @pl.when(low)
        def _():
            y_copy(z, ch).start()

    load_x1.wait()
    load_hv.wait()
    uext[taps:, :] = x1_ref[...] * hv_ref[...]

    @pl.when(high & has_up)
    def _():
        y_halo_high().start()

    load_pan.wait()
    half = pan_ref.shape[1] // 2
    gates = pan_ref[:, :half].astype(F32)
    hint[d] = (jax.nn.sigmoid(gates) * pan_ref[:, half:].astype(F32)).astype(BF16)
    eye = lax.broadcasted_iota(jnp.int32, (count, count), 0) == lax.broadcasted_iota(
        jnp.int32, (count, count), 1
    )
    steps = jnp.sum(
        jnp.where(eye, jnp.broadcast_to(step_ref[...], (count, count)), 0), axis=1, keepdims=True
    )
    code[d] = jnp.broadcast_to(own_ref[...] * seq + steps, (count, LANES))

    def hint_copy(s, me):
        return remote(
            hint.at[me], hint.at[me], hsend.at[s], hrecv.at[s], (c, (d + s) % n_dp)
        )

    def code_copy(s, me):
        return remote(
            code.at[me], code.at[me], csend.at[s], crecv.at[s], (c, (d + s) % n_dp)
        )

    for s in range(1, n_dp):
        hint_copy(s, d).start()
        code_copy(s, d).start()

    factor = HEAD_DIM ** -0.5 * math.log2(math.e)

    part_heads = kv_heads // CHUNKS

    def attend(block, ch, diagonal=False):
        slot = block * CHUNKS + ch

        def one(kh, carry):
            k_at = pl.ds(pl.multiple_of(kh * HEAD_DIM, HEAD_DIM), HEAD_DIM)
            v_at = pl.ds(pl.multiple_of(part_width + kh * HEAD_DIM, HEAD_DIM), HEAD_DIM)
            key = kv[slot, :, k_at]
            val = kv[slot, :, v_at]
            for g in range(grp):
                h = (ch * part_heads + kh) * grp + g
                query = q_ref[:, pl.ds(pl.multiple_of(h * HEAD_DIM, HEAD_DIM), HEAD_DIM)]
                score = lax.dot_general(
                    key, query, (((1,), (1,)), ((), ())), preferred_element_type=F32
                ) * factor
                if diagonal:
                    keep = lax.broadcasted_iota(jnp.int32, (tok, tok), 0) <= (
                        lax.broadcasted_iota(jnp.int32, (tok, tok), 1)
                    )
                    score = jnp.where(keep, score, NEG)
                    top = jnp.max(score, axis=0, keepdims=True)
                else:
                    before = m_ref[h]
                    top = jnp.maximum(before, jnp.max(score, axis=0, keepdims=True))
                expo = jnp.exp2(score - top)
                total = jnp.sum(expo, axis=0, keepdims=True)
                part = lax.dot_general(
                    val, expo.astype(BF16), (((0,), (0,)), ((), ())), preferred_element_type=F32
                )
                if diagonal:
                    l_ref[h] = total
                    o_ref[h] = part
                else:
                    shrink = jnp.exp2(before - top)
                    l_ref[h] = l_ref[h] * shrink + total
                    o_ref[h] = o_ref[h] * shrink + part
                m_ref[h] = top
            return carry

        lax.fori_loop(0, part_heads, one, 0)

    load_q.wait()
    for ch in range(CHUNKS):
        attend(c, ch, diagonal=True)

    @pl.when(low)
    def _():
        y_halo_low().start()

    lag_at = lax.broadcasted_iota(jnp.int32, (taps, 2 * taps), 0)
    col_at = lax.broadcasted_iota(jnp.int32, (taps, 2 * taps), 1)
    flip = jnp.where(lag_at == taps - col_at, 1.0, 0.0).astype(BF16)
    per_tile = LANES // chan
    n_tiles = width // LANES
    lane_group = lax.broadcasted_iota(jnp.int32, (taps, LANES), 1) // chan
    n_blk = tok // taps

    def pick(prod, col):
        res = prod[:taps, col]
        for g in range(1, per_tile):
            res = jnp.where(lane_group == g, prod[g * taps:(g + 1) * taps, col], res)
        return res

    def conv_tile(tile, carry):
        at = pl.ds(pl.multiple_of(tile * LANES, LANES), LANES)
        rows = filt_ref[pl.ds(pl.multiple_of(tile * per_tile, per_tile), per_tile), :]
        first = jnp.dot(rows, flip, preferred_element_type=F32)
        for g in range(per_tile):
            row = jnp.broadcast_to(first[g:g + 1, :], (taps, 2 * taps))
            toep[tile, g * taps:(g + 1) * taps, :] = pltpu.roll(
                row, 0, 1, stride=1, stride_axis=0
            ).astype(BF16)
        lower = toep[tile, :, taps:]
        prod = jnp.dot(lower, uext[taps:2 * taps, at], preferred_element_type=F32)
        conv[:taps, at] = pick(prod, slice(None))
        for b in range(1, n_blk):
            prod = jnp.dot(
                toep[tile], uext[b * taps:(b + 2) * taps, at], preferred_element_type=F32
            )
            conv[b * taps:(b + 1) * taps, at] = pick(prod, slice(None))
        return carry

    def step(i, carry):
        hi = z - 1 - i // CHUNKS
        ch = i % CHUNKS
        z_copy(hi, ch).wait_recv()

        @pl.when(has_up)
        def _():
            z_copy(hi, ch).start()

        @pl.when(high | (i >= CHUNKS))
        def _():
            y_copy(hi, ch).start()

        attend(2 * hi + y, ch)

        @pl.when((i >= 2 * CHUNKS) | (high & (i < CHUNKS)) | (low & (i >= CHUNKS)))
        def _():
            y_arrival(hi + 1, ch).wait_recv()
            attend(2 * (hi + 1) + 1 - y, ch)

        lax.fori_loop(i * n_tiles // (CHUNKS * z), (i + 1) * n_tiles // (CHUNKS * z), conv_tile, 0)
        return carry

    lax.fori_loop(0, CHUNKS * z, step, 0)

    @pl.when(z == 0)
    def _():
        lax.fori_loop(0, n_tiles, conv_tile, 0)

    @pl.when(low & has_up)
    def _():
        y_halo_high().wait_recv()
        z_extra_halo().start()

    @pl.when(high & has_up)
    def _():
        for ch in range(CHUNKS):
            @pl.when(z == 0)
            def _():
                y_arrival(z, ch).wait_recv()

            z_extra_block(z, ch).start()

    def conv_halo():
        def tile_step(tile, carry):
            at = pl.ds(pl.multiple_of(tile * LANES, LANES), LANES)
            prod = jnp.dot(
                toep[tile, :, :taps], uext[:taps, at], preferred_element_type=F32
            )
            conv[:taps, at] += pick(prod, slice(None))
            return carry

        lax.fori_loop(0, n_tiles, tile_step, 0)

    @pl.when(high)
    def _():
        y_halo_low().wait_recv()
        conv_halo()

    @pl.when((low & (z >= 1)) | (high & (z != 1)))
    def _():
        for ch in range(CHUNKS):
            @pl.when(z > 0)
            def _():
                y_arrival(0, ch).wait_recv()

            attend(1 - y, ch)

    @pl.when(low & has_down)
    def _():
        z_extra_halo().wait_recv()
        conv_halo()

    @pl.when(high & has_down)
    def _():
        for ch in range(CHUNKS):
            z_extra_block(z - 1, ch).wait_recv()
            attend(2 * (z - 1), ch)

    for s in range(1, n_dp):
        hint_copy(s, (d + n_dp - s) % n_dp).wait_recv()
        code_copy(s, (d + n_dp - s) % n_dp).wait_recv()

    load_x2.wait()
    spot = lax.broadcasted_iota(jnp.int32, (n_dp * count, tok), 1) + (d * seq + c * tok)
    codes = code[...].reshape(n_dp * count, LANES)[:, :1]
    landing = jnp.where(codes == spot, 1.0, 0.0).astype(BF16)
    for h in range(heads):
        at = pl.ds(h * HEAD_DIM, HEAD_DIM)
        placed = lax.dot_general(
            landing, hint[:, :, at].reshape(n_dp * count, HEAD_DIM),
            (((0,), (0,)), ((), ())), preferred_element_type=F32,
        )
        normed = (o_ref[h] / l_ref[h]).T
        out_ref[:, at] = (x2_ref[:, at].astype(F32) * conv[:, at] + normed + placed).astype(BF16)

    for s in range(1, n_dp):
        hint_copy(s, d).wait_send()
        code_copy(s, d).wait_send()

    @pl.when(low)
    def _():
        for ch in range(CHUNKS):
            y_copy(z, ch).wait_send()
        y_halo_low().wait_send()

    @pl.when(high & has_up)
    def _():
        y_halo_high().wait_send()
        for ch in range(CHUNKS):
            z_extra_block(z, ch).wait_send()

    @pl.when(low & has_up)
    def _():
        z_extra_halo().wait_send()

    @pl.when(has_up)
    def _():
        for ch in range(CHUNKS):
            z_copy(z, ch).wait_send()

    def drain(i, carry):
        hi = z - 1 - i // CHUNKS
        ch = i % CHUNKS

        @pl.when(has_up)
        def _():
            z_copy(hi, ch).wait_send()

        @pl.when(high | (i >= CHUNKS))
        def _():
            y_copy(hi, ch).wait_send()

        return carry

    lax.fori_loop(0, CHUNKS * z, drain, 0)


def solution(mesh):
    n_ctx, n_dp = mesh.shape["ctx"], mesh.shape["dp"]

    def per_device(q, k, v, x1, x2, hv, filters, panels, owner, step_rows):
        tok, width = q.shape[1:]
        kv_width = k.shape[2]
        heads = width // HEAD_DIM
        fgroups, taps = filters.shape
        count = panels.shape[1]
        n_sem = (n_ctx // 2 + 1) * CHUNKS
        dma = pltpu.SemaphoreType.DMA
        hbm = pl.BlockSpec(memory_space=pl.ANY)
        vmem = pl.BlockSpec(memory_space=pltpu.VMEM)
        out = pl.pallas_call(
            functools.partial(kernel, n_ctx, n_dp),
            out_shape=jax.ShapeDtypeStruct((tok, width), BF16),
            in_specs=[hbm] * 6 + [vmem, hbm, vmem, vmem],
            out_specs=vmem,
            scratch_shapes=[pltpu.VMEM((tok, width), BF16)] * 4 + [
                pltpu.VMEM((count, panels.shape[2]), BF16),
                pltpu.VMEM((n_ctx * CHUNKS, tok, 2 * kv_width // CHUNKS), BF16),
                pltpu.VMEM((taps + tok, width), BF16),
                pltpu.VMEM((taps, width), BF16),
                pltpu.VMEM((n_dp, count, width), BF16),
                pltpu.VMEM((n_dp, count, LANES), jnp.int32),
                pltpu.VMEM((width // LANES, taps * fgroups * LANES // width, 2 * taps), BF16),
                pltpu.VMEM((tok, width), F32),
                pltpu.VMEM((heads, 1, tok), F32),
                pltpu.VMEM((heads, 1, tok), F32),
                pltpu.VMEM((heads, HEAD_DIM, tok), F32),
                dma((n_sem,)), dma((n_sem,)), dma((n_sem,)), dma((n_sem,)),
                dma((n_dp,)), dma((n_dp,)), dma((n_dp,)), dma((n_dp,)), dma((2 * CHUNKS + 5,)),
            ],
            compiler_params=pltpu.CompilerParams(
                collective_id=0, has_side_effects=True, vmem_limit_bytes=56 * 2**20
            ),
        )(q[0], k[0], v[0], x1[0], x2[0], hv[0], filters, panels[0], owner[0], step_rows)
        return out[None]

    rows = P("dp", "ctx", None)
    return jax.shard_map(
        per_device,
        mesh=mesh,
        in_specs=(rows,) * 6 + (P(), rows, rows, P("dp", "ctx")),
        out_specs=rows,
        check_vma=False,
    )
```

```python
import functools
import math

import jax
import jax.numpy as jnp
from jax import lax
from jax.experimental import pallas as pl
from jax.experimental.pallas import tpu as pltpu
from jax.sharding import PartitionSpec as P

HEAD_DIM = 128
LANES = 128
NEG = -1e30
CHUNKS = 2
MESH = pl.DeviceIdType.MESH
F32 = jnp.float32
BF16 = jnp.bfloat16


def kernel(
    n_ctx, n_dp,
    q_hbm, k_hbm, v_hbm, x1_hbm, x2_hbm, hv_hbm, filt_ref, pan_hbm, own_ref, step_ref,
    out_ref,
    q_ref, x1_ref, x2_ref, hv_ref, pan_ref,
    kv, uext, hfwd, hint, code, toep, conv, land, m_ref, l_ref, o_ref,
    zsend, zrecv, ysend, yrecv, hsend, hrecv, csend, crecv, load_sem,
):
    tok, width = q_ref.shape
    kv_width = k_hbm.shape[1]
    part_width = kv_width // CHUNKS
    heads = width // HEAD_DIM
    kv_heads = kv_width // HEAD_DIM
    grp = heads // kv_heads
    fgroups, taps = filt_ref.shape
    chan = width // fgroups
    count = pan_ref.shape[0]
    seq = tok * n_ctx
    n_z = n_ctx // 2
    c = lax.axis_index("ctx")
    d = lax.axis_index("dp")
    z = c // 2
    y = c % 2
    low = y == 0
    high = y == 1
    has_up = z < n_z - 1
    has_down = z > 0
    partner = (2 * z + 1 - y, d)
    up = (jnp.minimum(c + 2, n_ctx - 1), d)
    down = (jnp.maximum(c - 2, 0), d)

    barrier = pltpu.get_barrier_semaphore()
    pl.semaphore_signal(barrier, 1, device_id=partner, device_id_type=MESH)
    for s in range(1, n_dp):
        pl.semaphore_signal(barrier, 1, device_id=(c, (d + s) % n_dp), device_id_type=MESH)

    @pl.when(has_up)
    def _():
        pl.semaphore_signal(barrier, 1, device_id=up, device_id_type=MESH)

    @pl.when(has_down)
    def _():
        pl.semaphore_signal(barrier, 1, device_id=down, device_id_type=MESH)

    def load(src, dst, index):
        return pltpu.make_async_copy(src, dst, load_sem.at[index])

    own_loads = []
    for ch in range(CHUNKS):
        cols = pl.ds(ch * part_width, part_width)
        own_loads.append((
            load(k_hbm.at[:, cols], kv.at[c * CHUNKS + ch, :, pl.ds(0, part_width)], 2 * ch),
            load(
                v_hbm.at[:, cols], kv.at[c * CHUNKS + ch, :, pl.ds(part_width, part_width)],
                2 * ch + 1,
            ),
        ))
    at_sem = 2 * CHUNKS
    load_x1 = load(x1_hbm, x1_ref, at_sem)
    load_hv = load(hv_hbm, hv_ref, at_sem + 1)
    load_pan = load(pan_hbm, pan_ref, at_sem + 2)
    load_q = load(q_hbm, q_ref, at_sem + 3)
    load_x2 = load(x2_hbm, x2_ref, at_sem + 4)
    for pair in own_loads:
        for one_load in pair:
            one_load.start()
    for one_load in (load_x1, load_hv, load_pan, load_q, load_x2):
        one_load.start()

    @pl.when(c == 0)
    def _():
        uext[:taps, :] = jnp.zeros((taps, width), BF16)

    pl.semaphore_wait(
        barrier, n_dp + has_up.astype(jnp.int32) + has_down.astype(jnp.int32)
    )

    def remote(src, dst, s_sem, r_sem, who):
        return pltpu.make_async_remote_copy(
            src_ref=src, dst_ref=dst, send_sem=s_sem, recv_sem=r_sem,
            device_id=who, device_id_type=MESH,
        )

    def z_copy(hi, ch):
        slot = kv.at[(2 * hi + y) * CHUNKS + ch]
        at = hi * CHUNKS + ch
        return remote(slot, slot, zsend.at[at], zrecv.at[at], up)

    last = n_z * CHUNKS

    def z_extra_block(hi, ch):
        slot = kv.at[2 * hi * CHUNKS + ch]
        return remote(slot, slot, zsend.at[last + ch], zrecv.at[last + ch], up)

    halo_out = uext.at[pl.ds(tok, taps)]
    halo_in = uext.at[pl.ds(0, taps)]

    def z_extra_halo():
        return remote(hfwd, halo_in, zsend.at[last], zrecv.at[last], up)

    def y_copy(hi, ch):
        slot = kv.at[(2 * hi + y) * CHUNKS + ch]
        at = hi * CHUNKS + ch
        return remote(slot, slot, ysend.at[at], yrecv.at[at], partner)

    def y_arrival(hi, ch):
        slot = kv.at[(2 * hi + 1 - y) * CHUNKS + ch]
        at = hi * CHUNKS + ch
        return remote(slot, slot, ysend.at[at], yrecv.at[at], partner)

    def y_halo_low():
        return remote(halo_out, halo_in, ysend.at[last], yrecv.at[last], partner)

    def y_halo_high():
        return remote(halo_out, hfwd, ysend.at[last], yrecv.at[last], partner)

    for ch in range(CHUNKS):
        for one_load in own_loads[ch]:
            one_load.wait()

        @pl.when(has_up)
        def _():
            z_copy(z, ch).start()

        @pl.when(low)
        def _():
            y_copy(z, ch).start()

    load_x1.wait()
    load_hv.wait()
    uext[taps:, :] = x1_ref[...] * hv_ref[...]

    @pl.when(high & has_up)
    def _():
        y_halo_high().start()

    load_pan.wait()
    half = pan_ref.shape[1] // 2
    gates = pan_ref[:, :half].astype(F32)
    hint[d] = (jax.nn.sigmoid(gates) * pan_ref[:, half:].astype(F32)).astype(BF16)
    eye = lax.broadcasted_iota(jnp.int32, (count, count), 0) == lax.broadcasted_iota(
        jnp.int32, (count, count), 1
    )
    steps = jnp.sum(
        jnp.where(eye, jnp.broadcast_to(step_ref[...], (count, count)), 0), axis=1, keepdims=True
    )
    code[d] = jnp.broadcast_to(own_ref[...] * seq + steps, (count, LANES))

    def hint_copy(s, me):
        return remote(
            hint.at[me], hint.at[me], hsend.at[s], hrecv.at[s], (c, (d + s) % n_dp)
        )

    def code_copy(s, me):
        return remote(
            code.at[me], code.at[me], csend.at[s], crecv.at[s], (c, (d + s) % n_dp)
        )

    for s in range(1, n_dp):
        hint_copy(s, d).start()
        code_copy(s, d).start()

    factor = HEAD_DIM ** -0.5 * math.log2(math.e)

    part_heads = kv_heads // CHUNKS

    def attend(block, ch, diagonal=False):
        slot = block * CHUNKS + ch

        def one(kh, carry):
            k_at = pl.ds(pl.multiple_of(kh * HEAD_DIM, HEAD_DIM), HEAD_DIM)
            v_at = pl.ds(pl.multiple_of(part_width + kh * HEAD_DIM, HEAD_DIM), HEAD_DIM)
            key = kv[slot, :, k_at]
            val = kv[slot, :, v_at]
            for g in range(grp):
                h = (ch * part_heads + kh) * grp + g
                query = q_ref[:, pl.ds(pl.multiple_of(h * HEAD_DIM, HEAD_DIM), HEAD_DIM)]
                score = lax.dot_general(
                    key, query, (((1,), (1,)), ((), ())), preferred_element_type=F32
                ) * factor
                if diagonal:
                    keep = lax.broadcasted_iota(jnp.int32, (tok, tok), 0) <= (
                        lax.broadcasted_iota(jnp.int32, (tok, tok), 1)
                    )
                    score = jnp.where(keep, score, NEG)
                    top = jnp.max(score, axis=0, keepdims=True)
                else:
                    before = m_ref[h]
                    top = jnp.maximum(before, jnp.max(score, axis=0, keepdims=True))
                expo = jnp.exp2(score - top)
                total = jnp.sum(expo, axis=0, keepdims=True)
                part = lax.dot_general(
                    val, expo.astype(BF16), (((0,), (0,)), ((), ())), preferred_element_type=F32
                )
                if diagonal:
                    l_ref[h] = total
                    o_ref[h] = part
                else:
                    shrink = jnp.exp2(before - top)
                    l_ref[h] = l_ref[h] * shrink + total
                    o_ref[h] = o_ref[h] * shrink + part
                m_ref[h] = top
            return carry

        lax.fori_loop(0, part_heads, one, 0)

    load_q.wait()
    for ch in range(CHUNKS):
        attend(c, ch, diagonal=True)

    @pl.when(low)
    def _():
        y_halo_low().start()

    lag_at = lax.broadcasted_iota(jnp.int32, (taps, 2 * taps), 0)
    col_at = lax.broadcasted_iota(jnp.int32, (taps, 2 * taps), 1)
    flip = jnp.where(lag_at == taps - col_at, 1.0, 0.0).astype(BF16)
    per_tile = LANES // chan
    n_tiles = width // LANES
    lane_group = lax.broadcasted_iota(jnp.int32, (taps, LANES), 1) // chan
    n_blk = tok // taps

    def pick(prod, col):
        res = prod[:taps, col]
        for g in range(1, per_tile):
            res = jnp.where(lane_group == g, prod[g * taps:(g + 1) * taps, col], res)
        return res

    def conv_tile(tile, carry):
        at = pl.ds(pl.multiple_of(tile * LANES, LANES), LANES)
        rows = filt_ref[pl.ds(pl.multiple_of(tile * per_tile, per_tile), per_tile), :]
        first = jnp.dot(rows, flip, preferred_element_type=F32)
        for g in range(per_tile):
            row = jnp.broadcast_to(first[g:g + 1, :], (taps, 2 * taps))
            toep[tile, g * taps:(g + 1) * taps, :] = pltpu.roll(
                row, 0, 1, stride=1, stride_axis=0
            ).astype(BF16)
        lower = toep[tile, :, taps:]
        prod = jnp.dot(lower, uext[taps:2 * taps, at], preferred_element_type=F32)
        conv[:taps, at] = pick(prod, slice(None))
        for b in range(1, n_blk):
            prod = jnp.dot(
                toep[tile], uext[b * taps:(b + 2) * taps, at], preferred_element_type=F32
            )
            conv[b * taps:(b + 1) * taps, at] = pick(prod, slice(None))
        return carry

    def step(i, carry):
        hi = z - 1 - i // CHUNKS
        ch = i % CHUNKS
        z_copy(hi, ch).wait_recv()

        @pl.when(has_up)
        def _():
            z_copy(hi, ch).start()

        @pl.when(high | (i >= CHUNKS))
        def _():
            y_copy(hi, ch).start()

        attend(2 * hi + y, ch)

        @pl.when((i >= 2 * CHUNKS) | (high & (i < CHUNKS)) | (low & (i >= CHUNKS)))
        def _():
            y_arrival(hi + 1, ch).wait_recv()
            attend(2 * (hi + 1) + 1 - y, ch)

        lax.fori_loop(i * n_tiles // (CHUNKS * z), (i + 1) * n_tiles // (CHUNKS * z), conv_tile, 0)
        return carry

    lax.fori_loop(0, CHUNKS * z, step, 0)

    @pl.when(z == 0)
    def _():
        lax.fori_loop(0, n_tiles, conv_tile, 0)

    @pl.when(low & has_up)
    def _():
        y_halo_high().wait_recv()
        z_extra_halo().start()

    @pl.when(high & has_up)
    def _():
        for ch in range(CHUNKS):
            @pl.when(z == 0)
            def _():
                y_arrival(z, ch).wait_recv()

            z_extra_block(z, ch).start()

    for s in range(1, n_dp):
        hint_copy(s, (d + n_dp - s) % n_dp).wait_recv()
        code_copy(s, (d + n_dp - s) % n_dp).wait_recv()

    spot = lax.broadcasted_iota(jnp.int32, (n_dp * count, tok), 1) + (d * seq + c * tok)
    codes = code[...].reshape(n_dp * count, LANES)[:, :1]
    landing = jnp.where(codes == spot, 1.0, 0.0).astype(BF16)
    for h in range(heads):
        at = pl.ds(h * HEAD_DIM, HEAD_DIM)
        land[:, at] = lax.dot_general(
            landing, hint[:, :, at].reshape(n_dp * count, HEAD_DIM),
            (((0,), (0,)), ((), ())), preferred_element_type=F32,
        )

    def conv_halo():
        def tile_step(tile, carry):
            at = pl.ds(pl.multiple_of(tile * LANES, LANES), LANES)
            prod = jnp.dot(
                toep[tile, :, :taps], uext[:taps, at], preferred_element_type=F32
            )
            conv[:taps, at] += pick(prod, slice(None))
            return carry

        lax.fori_loop(0, n_tiles, tile_step, 0)

    @pl.when(high)
    def _():
        y_halo_low().wait_recv()
        conv_halo()

    @pl.when((low & (z >= 1)) | (high & (z != 1)))
    def _():
        for ch in range(CHUNKS):
            @pl.when(z > 0)
            def _():
                y_arrival(0, ch).wait_recv()

            attend(1 - y, ch)

    @pl.when(low & has_down)
    def _():
        z_extra_halo().wait_recv()
        conv_halo()

    @pl.when(high & has_down)
    def _():
        for ch in range(CHUNKS):
            z_extra_block(z - 1, ch).wait_recv()
            attend(2 * (z - 1), ch)

    load_x2.wait()
    for h in range(heads):
        at = pl.ds(h * HEAD_DIM, HEAD_DIM)
        normed = (o_ref[h] * (1.0 / l_ref[h])).T
        out_ref[:, at] = (
            x2_ref[:, at].astype(F32) * conv[:, at] + normed + land[:, at]
        ).astype(BF16)

    for s in range(1, n_dp):
        hint_copy(s, d).wait_send()
        code_copy(s, d).wait_send()

    @pl.when(low)
    def _():
        for ch in range(CHUNKS):
            y_copy(z, ch).wait_send()
        y_halo_low().wait_send()

    @pl.when(high & has_up)
    def _():
        y_halo_high().wait_send()
        for ch in range(CHUNKS):
            z_extra_block(z, ch).wait_send()

    @pl.when(low & has_up)
    def _():
        z_extra_halo().wait_send()

    @pl.when(has_up)
    def _():
        for ch in range(CHUNKS):
            z_copy(z, ch).wait_send()

    def drain(i, carry):
        hi = z - 1 - i // CHUNKS
        ch = i % CHUNKS

        @pl.when(has_up)
        def _():
            z_copy(hi, ch).wait_send()

        @pl.when(high | (i >= CHUNKS))
        def _():
            y_copy(hi, ch).wait_send()

        return carry

    lax.fori_loop(0, CHUNKS * z, drain, 0)


def solution(mesh):
    n_ctx, n_dp = mesh.shape["ctx"], mesh.shape["dp"]

    def per_device(q, k, v, x1, x2, hv, filters, panels, owner, step_rows):
        tok, width = q.shape[1:]
        kv_width = k.shape[2]
        heads = width // HEAD_DIM
        fgroups, taps = filters.shape
        count = panels.shape[1]
        n_sem = (n_ctx // 2 + 1) * CHUNKS
        dma = pltpu.SemaphoreType.DMA
        hbm = pl.BlockSpec(memory_space=pl.ANY)
        vmem = pl.BlockSpec(memory_space=pltpu.VMEM)
        out = pl.pallas_call(
            functools.partial(kernel, n_ctx, n_dp),
            out_shape=jax.ShapeDtypeStruct((tok, width), BF16),
            in_specs=[hbm] * 6 + [vmem, hbm, vmem, vmem],
            out_specs=vmem,
            scratch_shapes=[pltpu.VMEM((tok, width), BF16)] * 4 + [
                pltpu.VMEM((count, panels.shape[2]), BF16),
                pltpu.VMEM((n_ctx * CHUNKS, tok, 2 * kv_width // CHUNKS), BF16),
                pltpu.VMEM((taps + tok, width), BF16),
                pltpu.VMEM((taps, width), BF16),
                pltpu.VMEM((n_dp, count, width), BF16),
                pltpu.VMEM((n_dp, count, LANES), jnp.int32),
                pltpu.VMEM((width // LANES, taps * fgroups * LANES // width, 2 * taps), BF16),
                pltpu.VMEM((tok, width), F32),
                pltpu.VMEM((tok, width), F32),
                pltpu.VMEM((heads, 1, tok), F32),
                pltpu.VMEM((heads, 1, tok), F32),
                pltpu.VMEM((heads, HEAD_DIM, tok), F32),
                dma((n_sem,)), dma((n_sem,)), dma((n_sem,)), dma((n_sem,)),
                dma((n_dp,)), dma((n_dp,)), dma((n_dp,)), dma((n_dp,)), dma((2 * CHUNKS + 5,)),
            ],
            compiler_params=pltpu.CompilerParams(
                collective_id=0, has_side_effects=True, vmem_limit_bytes=56 * 2**20
            ),
        )(q[0], k[0], v[0], x1[0], x2[0], hv[0], filters, panels[0], owner[0], step_rows)
        return out[None]

    rows = P("dp", "ctx", None)
    return jax.shard_map(
        per_device,
        mesh=mesh,
        in_specs=(rows,) * 6 + (P(), rows, rows, P("dp", "ctx")),
        out_specs=rows,
        check_vma=False,
    )
```
